128 devices in a mesh: dp: 8 (over y, z_lo), tok: 16 (over x, z_hi, core).
Axes of the slice: x: 4, y: 4, z: 4 (z_hi: 2, z_lo: 2; z = z_hi * 2 + z_lo), core: 2. Of those that a mesh axis runs over, the one named last changes fastest.
Arguments:
- embeddings: bfloat16 [2560, 1024, 256], P('dp', 'tok'), may hold values from -6 to 6
- projection: bfloat16 [1024, 32], P('tok'), may hold values from -0.01171875 to 0.01171875
- mlp_weight: bfloat16 [32768, 1024], P('tok'), may hold values from -0.03125 to 0.03125
- mlp_bias: float32 [1024], replicated, may hold values from -1 to 1
- upstream: bfloat16 [2560, 1024], P('dp'), may hold values from -24 to 24
Outputs:
- grad_embeddings: bfloat16 [2560, 1024, 256], P('dp', 'tok')
- grad_weight: float32 [32768, 1024], P(('tok', 'dp'))
- grad_projection: float32 [1024, 32], P('tok')
- grad_bias: float32 [1024], replicated
The draws below stay inside these ranges and needn't reach their ends.
All inputs are finite; a program needn't handle non-finite values.
Results may differ from the reference program's by a relative error of at most 0.034.
Values may be sent and summed in bfloat16 or wider, within the bound.
No kernel may reach another device: no remote copies, remote signals or barrier semaphores. Data moves between devices by JAX's collectives and lax.ppermute only.
A program may use at most 192 MiB of HBM per device.

```python
import jax
import jax.numpy as jnp
from jax import lax

D = 256
N_EMB = 1024
K = 32
H = 1024
EX_DEV = 320
EXAMPLES = 2560
TOK_DEV = 64


def shard_levels(rng, extent, shards, low, high):
    factor_of, own = 1.0, jax.random.fold_in(rng, 6)
    for axis_at, shards_of in shards:
        draws = jnp.exp(jax.random.uniform(jax.random.fold_in(own, axis_at), (shards_of,), jnp.float32, low / len(shards), high / len(shards)))
        factor_of = factor_of * jnp.repeat(draws, extent[axis_at] // shards_of).reshape([-1 if axis == axis_at else 1 for axis in range(len(extent))])
    return factor_of


def bell_draw(key, dims, scale, most, split=(), dtype=jnp.bfloat16):
    entries = jax.random.normal(key, dims, jnp.float32) * scale
    if len(split) > 0:
        entries = shard_levels(key, dims, split, -0.22, 0.18) * entries
    return jnp.clip(entries, min=-most, max=most).astype(dtype)


def setup_inputs(seed: int = 0) -> dict:
    key_list = jax.random.split(jax.random.key(seed), 6)
    embeddings = bell_draw(key_list[0], (EXAMPLES, N_EMB, D), 1.0, 6.0, ((0, 8), (1, 16)))
    projection = bell_draw(key_list[1], (N_EMB, K), (N_EMB * D) ** -0.5, 0.01171875, ((0, 16),))
    mlp_weight = bell_draw(key_list[2], (N_EMB * K, H), (N_EMB * K) ** -0.5, 0.03125, ((0, 16),))
    mlp_bias = jnp.clip(jax.random.uniform(key_list[3], (H,), jnp.float32, -1.0, 1.0), -1.0, 1.0)
    upstream = bell_draw(key_list[4], (EXAMPLES, H), 4.0, 24.0, ((0, 8),))
    return {"embeddings": embeddings, "projection": projection, "mlp_weight": mlp_weight, "mlp_bias": mlp_bias, "upstream": upstream}


def silu_grad(value):
    sig = jax.nn.sigmoid(value)
    return sig * (1.0 + value * (1.0 - sig))

def reference(embeddings, projection, mlp_weight, mlp_bias, upstream):
    blocks = N_EMB // TOK_DEV
    count = EXAMPLES // EX_DEV
    proj32 = projection.astype(jnp.float32)
    proj_groups = proj32.reshape(blocks, TOK_DEV, K)
    weight32 = mlp_weight.astype(jnp.float32)
    weight_groups = weight32.reshape(blocks, TOK_DEV * K, H)
    xs_all = embeddings.reshape(count, EX_DEV, N_EMB, D)
    gs_all = upstream.reshape(count, EX_DEV, H)

    def step(carry, pieces):
        grad_w, grad_p, grad_b = carry
        xblock, gblock = pieces
        x32 = xblock.astype(jnp.float32)
        xgroups = x32.reshape(EX_DEV, blocks, TOK_DEV, D)
        part = jnp.einsum('gtk,egtd->egkd', proj_groups, xgroups)
        compressed = lax.optimization_barrier(jnp.sum(part.astype(jnp.bfloat16).astype(jnp.float32), axis=1))
        comp_b = compressed.astype(jnp.bfloat16)
        field = jnp.einsum('end,ekd->enk', x32, comp_b.astype(jnp.float32)).astype(jnp.bfloat16)
        flat = field.reshape(EX_DEV, N_EMB * K)
        fgroups = flat.astype(jnp.float32).reshape(EX_DEV, blocks, TOK_DEV * K)
        hpart = jnp.einsum('egr,grh->egh', fgroups, weight_groups)
        pre = lax.optimization_barrier(jnp.sum(hpart.astype(jnp.bfloat16).astype(jnp.float32), axis=1)) + mlp_bias
        grad_pre = (gblock.astype(jnp.float32) * silu_grad(pre)).astype(jnp.bfloat16)
        grad_b = grad_b + lax.optimization_barrier(jnp.sum(grad_pre.astype(jnp.float32), axis=0))
        grad_w = grad_w + lax.dot_general(flat, grad_pre, (((0,), (0,)), ((), ())), preferred_element_type=jnp.float32)
        dflat = lax.dot_general(grad_pre, mlp_weight, (((1,), (1,)), ((), ())), preferred_element_type=jnp.float32).astype(jnp.bfloat16)
        dfield = dflat.astype(jnp.float32).reshape(EX_DEV, N_EMB, K)
        dgroups = dfield.reshape(EX_DEV, blocks, TOK_DEV, K)
        dpart = jnp.einsum('egtk,egtd->egkd', dgroups, xgroups)
        dcomp = lax.optimization_barrier(jnp.sum(dpart.astype(jnp.bfloat16).astype(jnp.float32), axis=1)).astype(jnp.bfloat16)
        dcomp32 = dcomp.astype(jnp.float32)
        grad_x = jnp.einsum('enk,ekd->end', dfield, comp_b.astype(jnp.float32)) + jnp.einsum('nk,ekd->end', proj32, dcomp32)
        grad_p = grad_p + jnp.einsum('end,ekd->nk', x32, dcomp32)
        return ((grad_w, grad_p, grad_b), grad_x.astype(jnp.bfloat16))
    init = (jnp.zeros((N_EMB * K, H), jnp.float32), jnp.zeros((N_EMB, K), jnp.float32), jnp.zeros((H,), jnp.float32))
    (grad_w, grad_p, grad_b), grad_x = lax.scan(step, init, (xs_all, gs_all))
    return (grad_x.reshape(EXAMPLES, N_EMB, D), grad_w, grad_p, grad_b)
```

```python
import jax, jax.numpy as jnp
from jax import lax
from jax.experimental import pallas as pl
from jax.experimental.pallas import tpu as pltpu
from jax.sharding import PartitionSpec as P
f32=jnp.float32; bf=jnp.bfloat16
EB=16
T,K,D,H=64,32,256,1024
VM=pltpu.CompilerParams(vmem_limit_bytes=32*1024*1024)
def whole(shape): return pl.BlockSpec(shape, lambda i,*_: (0,)*len(shape))
def xspec(): return pl.BlockSpec((EB,T,D), lambda i,tbl,blk: (blk[0]+i,0,0))

def k1_body(tbl, blk, x, pt4, out):
    i=pl.program_id(0)
    for g in range(EB//4):
        r=jnp.dot(pt4[...], x[4*g:4*g+4].reshape(4*T,D), preferred_element_type=f32).astype(bf)
        for j in range(4):
            out[tbl[i*EB+4*g+j]]=r[K*j:K*j+K]
def k1(x,pt4,tbl,blk):
    n=tbl.shape[0]
    return pl.pallas_call(k1_body, out_shape=jax.ShapeDtypeStruct((n,K,D),bf),
        grid_spec=pltpu.PrefetchScalarGridSpec(num_scalar_prefetch=2, grid=(n//EB,),
            in_specs=[xspec(), whole((4*K,4*T))], out_specs=whole((n,K,D))),
        compiler_params=VM, name="compress")(tbl,blk,x,pt4)

def k2_body(tbl, blk, perm, x, comp, flat, flatp, sc):
    i=pl.program_id(0)
    for e in range(EB):
        c=comp[tbl[i*EB+e]]
        c4=jnp.concatenate([c]*4,axis=0)
        sc[T*e:T*e+T,:]=lax.dot_general(x[e],c4,(((1,),(1,)),((),())),preferred_element_type=f32)
    lane=lax.broadcasted_iota(jnp.int32,(EB,128),1)>>5
    for g in range(T//4):
        acc=sc[pl.ds(4*g,EB,stride=T),:]
        for j in range(1,4):
            acc=jnp.where(lane==j, sc[pl.ds(4*g+j,EB,stride=T),:], acc)
        flat[:,128*g:128*g+128]=acc.astype(bf)
    for j in range(8):
        flatp[:,256*j:256*j+256]=flat[:,pl.ds(pl.multiple_of(perm[j]*256,256),256)]
def k2(x,comp,tbl,blk,perm):
    n=tbl.shape[0]
    fs=pl.BlockSpec((EB,T*K), lambda i,*_: (i,0))
    return pl.pallas_call(k2_body, out_shape=[jax.ShapeDtypeStruct((n,T*K),bf)]*2,
        grid_spec=pltpu.PrefetchScalarGridSpec(num_scalar_prefetch=3, grid=(n//EB,),
            in_specs=[pl.BlockSpec((EB,T,D), lambda i,tbl,blk,perm: (blk[0]+i,0,0)), whole((n,K,D))], out_specs=[fs,fs],
            scratch_shapes=[pltpu.VMEM((EB*T,128),f32)]),
        compiler_params=VM, name="field")(tbl,blk,perm,x,comp)

def expand(df, sc):
    lane=lax.broadcasted_iota(jnp.int32,(EB,128),1)>>5
    for g in range(T//4):
        v=df[:,128*g:128*g+128].astype(f32)
        for j in range(4):
            sc[pl.ds(4*g+j,EB,stride=T),:]=jnp.where(lane==j,v,0.0)

def k3_body(tbl, blk, x, df, out, sc):
    i=pl.program_id(0)
    expand(df,sc)
    for e in range(EB):
        s=sc[T*e:T*e+T,:].astype(bf)
        r=lax.dot_general(s,x[e],(((0,),(0,)),((),())),preferred_element_type=f32)
        out[tbl[i*EB+e]]=(r[:K]+r[K:2*K]+r[2*K:3*K]+r[3*K:]).astype(bf)
def k3(x,df,tbl,blk):
    n=tbl.shape[0]
    return pl.pallas_call(k3_body, out_shape=jax.ShapeDtypeStruct((n,K,D),bf),
        grid_spec=pltpu.PrefetchScalarGridSpec(num_scalar_prefetch=2, grid=(n//EB,),
            in_specs=[xspec(), pl.BlockSpec((EB,T*K), lambda i,*_: (i,0))], out_specs=whole((n,K,D)),
            scratch_shapes=[pltpu.VMEM((EB*T,128),f32)]),
        compiler_params=VM, name="grad_compress")(tbl,blk,x,df)

def k4_body(tbl, blk, df, comp, dcomp, pexp, gx_in, gx, sc):
    i=pl.program_id(0)
    expand(df,sc)
    p=pexp[...]
    for e in range(EB):
        s=jnp.concatenate([sc[T*e:T*e+T,:].astype(bf),p],axis=1)
        c=comp[tbl[i*EB+e]]; d=dcomp[tbl[i*EB+e]]
        w=jnp.concatenate([c]*4+[d]*4,axis=0)
        gx[e]=jnp.dot(s,w,preferred_element_type=f32).astype(bf)
def k4(df,comp,dcomp,pexp,gx,shape,tbl,blk):
    n=tbl.shape[0]
    in_specs=[pl.BlockSpec((EB,T*K), lambda i,*_: (i,0)), whole((n,K,D)), whole((n,K,D)), whole((T,128))]
    args=[df,comp,dcomp,pexp]
    body=k4_body; alias={}
    if gx is None:
        def body(tbl, blk, df, comp, dcomp, pexp, gx, sc): k4_body(tbl,blk,df,comp,dcomp,pexp,None,gx,sc)
    else:
        in_specs.append(pl.BlockSpec(memory_space=pl.ANY)); args.append(gx); alias={6:0}
    return pl.pallas_call(body, out_shape=jax.ShapeDtypeStruct(shape,bf),
        grid_spec=pltpu.PrefetchScalarGridSpec(num_scalar_prefetch=2, grid=(n//EB,),
            in_specs=in_specs, out_specs=xspec(),
            scratch_shapes=[pltpu.VMEM((EB*T,128),f32)]),
        input_output_aliases=alias,
        compiler_params=VM, name="grad_tokens")(tbl,blk,*args)

def k5_body(tbl, blk, x, dcomp, gp):
    i=pl.program_id(0)
    @pl.when(i==0)
    def _(): gp[...]=jnp.zeros_like(gp)
    acc=gp[...]
    for e in range(EB):
        acc=acc+lax.dot_general(dcomp[tbl[i*EB+e]],x[e],(((1,),(1,)),((),())),preferred_element_type=f32)
    gp[...]=acc
def k5(x,dcomp,tbl,blk):
    n=tbl.shape[0]
    return pl.pallas_call(k5_body, out_shape=jax.ShapeDtypeStruct((K,T),f32),
        grid_spec=pltpu.PrefetchScalarGridSpec(num_scalar_prefetch=2, grid=(n//EB,),
            in_specs=[xspec(), whole((n,K,D))], out_specs=whole((K,T))),
        compiler_params=VM, name="grad_projection")(tbl,blk,x,dcomp)


NCH = 2
ORDERS = (("ABZ", "BAZ"), ("ABZ", "BAZ"))
DP_ORDERS = ("ABZ", "BAZ")


def tok_bits(i):
    x = i // 4
    g = x ^ (x >> 1)
    return {"A": g & 1, "B": g >> 1, "Z": (i >> 1) & 1}


def tok_flip(i, d):
    x = i // 4
    return {"A": (x ^ 1) * 4 + i % 4, "B": (3 - x) * 4 + i % 4, "Z": i ^ 2, "C": i ^ 1}[d]


def dp_bits(i):
    y = i // 2
    g = y ^ (y >> 1)
    return {"A": g & 1, "B": g >> 1, "Z": i & 1}


def dp_flip(i, d):
    y = i // 2
    return {"A": (y ^ 1) * 2 + i % 2, "B": (3 - y) * 2 + i % 2, "Z": i ^ 1}[d]


def place(bits, order):
    return bits[order[0]] * 4 + bits[order[1]] * 2 + bits[order[2]]


def tok_swap(x, step, orders):
    if step == "C":
        pairs = [(i, tok_flip(i, "C")) for i in range(16)]
    else:
        pairs = [(i, tok_flip(i, orders[i & 1][step])) for i in range(16)]
    return lax.ppermute(x, "tok", pairs)


def dp_swap(x, step):
    pairs = []
    for d in range(8):
        for t in range(16):
            pairs.append((d * 16 + t, dp_flip(d, DP_ORDERS[t & 1][step]) * 16 + t))
    return lax.ppermute(x, ("dp", "tok"), pairs)


def add(a, b, dtype=jnp.bfloat16):
    return (a.astype(jnp.float32) + b.astype(jnp.float32)).astype(dtype)


def reduce_scatter(x, got, swap):
    for step in range(3):
        h = x.shape[0] // 2
        if got is None:
            keep, send = x[:h], x[h:]
        else:
            keep, send = add(x[:h], got[:h]), add(x[h:], got[h:])
        got = swap(send, step)
        x = keep
    return x, got


def all_gather(x, swap):
    for step in (2, 1, 0):
        x = jnp.concatenate([x, swap(x, step)], axis=0)
    return x


def all_sum(x, swap):
    for step in range(3):
        x = add(x, swap(x, step), x.dtype)
    return x


def silu_grad(value):
    sig = jax.nn.sigmoid(value)
    return sig * (1.0 + value * (1.0 - sig))


def per_device(embeddings, projection, mlp_weight, mlp_bias, upstream):
    examples = embeddings.shape[0]
    half = examples // NCH // 2
    part = half // 8
    tok = lax.axis_index("tok")
    dp = lax.axis_index("dp")
    core = tok & 1
    bits = tok_bits(tok)
    dbits = dp_bits(dp)
    own = jnp.where(core == 0, place(dbits, DP_ORDERS[0]), place(dbits, DP_ORDERS[1]))
    owners = []
    for order in DP_ORDERS:
        table = [0] * 8
        for d in range(8):
            table[place(dp_bits(d), order)] = d
        owners.append(table)
    owners = jnp.asarray(owners, jnp.int32)[core]
    perm = owners[own ^ jnp.arange(8)].astype(jnp.int32)

    pt4 = jnp.kron(jnp.eye(4, dtype=bf), projection.T)
    lanes = (jnp.arange(128)[None] // K) == (jnp.arange(T)[:, None] % 4)
    pexp = jnp.where(lanes, jnp.tile(projection, (1, 4)), 0).astype(bf)

    e = jnp.arange(half, dtype=jnp.int32)
    tables, blocks, swaps = [], [], []
    for c in range(NCH):
        orders = ORDERS[c]
        tabs = [((e // part) ^ place(bits, orders[h])) * part + e % part for h in range(2)]
        tables.append((jnp.where(core == 0, tabs[0], tabs[1]), jnp.where(core == 0, tabs[1], tabs[0])))
        first = c * 2 * half // EB
        blocks.append(((first + core * (half // EB)).reshape(1), (first + (1 - core) * (half // EB)).reshape(1)))
        swaps.append(lambda x, step, orders=orders: tok_swap(x, step, orders))

    def total(c, kernel):
        other = kernel(1)
        got = swaps[c](other, "C")
        mine = kernel(0)
        x = all_gather(add(*reduce_scatter(mine, got, swaps[c])), swaps[c])
        return x, swaps[c](x, "C")

    comp, dcomp, flat, flatp, gpre = [], [], [], [], []
    for c in range(NCH):
        with jax.named_scope("compressed"):
            comp.append(total(c, lambda h: k1(embeddings, pt4, tables[c][h], blocks[c][h])))
    for c in range(NCH):
        with jax.named_scope("pre"):
            fl, flp, hp = [None, None], [None, None], [None, None]
            for h in (0, 1):
                fl[h], flp[h] = k2(embeddings, comp[c][h], tables[c][h], blocks[c][h], perm)
                hp[h] = jnp.dot(fl[h], mlp_weight, preferred_element_type=f32).astype(bf)
            x = add(hp[0], swaps[c](hp[1], "C"))
            x = all_sum(x, swaps[c])
            pre = [x, swaps[c](x, "C")]
            up = upstream.reshape(NCH, 2, half, H)[c]
            gp = []
            for h in (0, 1):
                u = lax.dynamic_index_in_dim(up, core if h == 0 else 1 - core, 0, keepdims=False)
                gp.append((u.astype(f32) * silu_grad(pre[h].astype(f32) + mlp_bias)).astype(bf))
            flat.append(fl)
            flatp.append(flp)
            gpre.append(gp)
    dflat = []
    for c in range(NCH):
        with jax.named_scope("grad_compressed"):
            df = [
                lax.dot_general(g, mlp_weight, (((1,), (1,)), ((), ())), preferred_element_type=f32).astype(bf)
                for g in gpre[c]
            ]
            dflat.append(df)
            dcomp.append(total(c, lambda h: k3(embeddings, df[h], tables[c][h], blocks[c][h])))
    with jax.named_scope("grad_weight"):
        rows = jnp.concatenate([f for fs in flatp for f in fs], axis=0)
        cols = jnp.concatenate([g for gs in gpre for g in gs], axis=0)
        gw = lax.dot_general(rows, cols, (((0,), (0,)), ((), ())), preferred_element_type=f32).astype(bf)
        a, b = reduce_scatter(gw, None, dp_swap)
        grad_w = a.astype(f32) + b.astype(f32)
        bias = jnp.sum(cols.astype(f32), axis=0)
    with jax.named_scope("grad_projection"):
        gp = sum(k5(embeddings, dcomp[c][h], tables[c][h], blocks[c][h]) for c in range(NCH) for h in (0, 1))
        both = jnp.concatenate([gp.reshape(T * K // 128, 128), bias.reshape(H // 128, 128)], axis=0)
        both = all_sum(both, dp_swap)
        grad_p = both[: T * K // 128].reshape(K, T).T
        grad_b = both[T * K // 128 :].reshape(H)
    with jax.named_scope("grad_embeddings"):
        gx = None
        for c in range(NCH):
            for h in (0, 1):
                gx = k4(dflat[c][h], comp[c][h], dcomp[c][h], pexp, gx, embeddings.shape, tables[c][h], blocks[c][h])
    return gx, grad_w, grad_p, grad_b


def solution(mesh):
    in_specs = (P("dp", "tok", None), P("tok", None), P("tok", None), P(), P("dp", None))
    out_specs = (P("dp", "tok", None), P(("tok", "dp"), None), P("tok", None), P())
    return jax.shard_map(
        per_device, mesh=mesh, in_specs=in_specs, out_specs=out_specs, check_vma=False
    )
```

```python
import jax
import jax.numpy as jnp
from jax import lax
from jax.experimental import pallas as pl
from jax.experimental.pallas import tpu as pltpu
from jax.sharding import PartitionSpec as P

f32 = jnp.float32
bf = jnp.bfloat16
T, K, D, H = 64, 32, 256, 1024
EB = 16
NCH = 2
ORDERS = (("ABZ", "BAZ"), ("ABZ", "BAZ"))
DP_ORDERS = ("ABZ", "BAZ")
ORDER = (
    1, 1, 1, 0, 0, 0, 1, 0, 1, 0, 1, 0, 1, 0, 1, 0, 1, 1, 1, 0,
    0, 1, 0, 1, 0, 1, 0, 1, 0, 1, 1, 0, 1, 0, 0, 1, 0, 1, "w", 0,
    1, 0, 1, 0, 1, 0, "w", 1, 1, 0, 1, 1, 1, 0, 0, 0, "s", "w", "s", 0,
    "s", 0, "w", "s",
)


class Chain:
    def __init__(self):
        self.last = []


def call(chain, body, name, outs, scratch, smem=(), vmem=(), far=(), alias=None):
    specs = [pl.BlockSpec(memory_space=pltpu.SMEM)] * len(smem)
    specs += [pl.BlockSpec(memory_space=pltpu.VMEM)] * len(vmem)
    specs += [pl.BlockSpec(memory_space=pl.ANY)] * (len(far) + len(chain.last))
    vmem = [pltpu.with_memory_space_constraint(a, pltpu.VMEM) if a.size > 100000 else a for a in vmem]
    far = [pltpu.with_memory_space_constraint(a, pltpu.HBM) for a in far]
    ins, skip = len(smem) + len(vmem) + len(far), len(chain.last)

    def run(*refs):
        body(*refs[:ins], *refs[ins + skip :])

    def place(out):
        return pl.BlockSpec(memory_space=pltpu.VMEM if isinstance(out, jax.ShapeDtypeStruct) else pl.ANY)

    result = pl.pallas_call(
        run,
        out_shape=outs,
        in_specs=specs,
        out_specs=[place(out) for out in outs],
        scratch_shapes=scratch,
        input_output_aliases=alias or {},
        compiler_params=pltpu.CompilerParams(vmem_limit_bytes=8 * 1024 * 1024),
        name=name,
    )(*smem, *vmem, *far, *chain.last)
    chain.last = [result[-1]]
    return result


def shape(*dims, dtype=bf):
    return jax.ShapeDtypeStruct(dims, dtype)


def compress(chain, x, pt4, tbl, blk):
    n = tbl.shape[0]

    def body(tbl, blk, pt4, x, xv, out, sem):
        def copy(i):
            return pltpu.make_async_copy(x.at[pl.ds((blk[0] + i) * EB, EB)], xv.at[pl.ds(i * EB, EB)], sem.at[i])

        for i in range(n // EB):
            copy(i).start()

        @pl.loop(0, n // EB)
        def _(i):
            copy(i).wait()
            for g in range(EB // 4):
                x4 = xv[pl.ds(i * EB + 4 * g, 4)].reshape(4 * T, D)
                r = jnp.dot(pt4[...], x4, preferred_element_type=f32).astype(bf)
                for j in range(4):
                    out[tbl[i * EB + 4 * g + j]] = r[K * j : K * j + K]

    outs = [shape(n, T, D), shape(n, K, D)]
    return call(chain, body, "compress", outs, [pltpu.SemaphoreType.DMA((n // EB,))], [tbl, blk], [pt4], [x])


def field(chain, x, comp, w, tbl, perm):
    n = tbl.shape[0]

    def body(tbl, perm, comp, x, w, flatp, hidden, sc, flat):
        lane = lax.broadcasted_iota(jnp.int32, (EB, 128), 1) // K

        @pl.loop(0, n // EB)
        def _(i):
            for e in range(EB):
                c = comp[tbl[i * EB + e]]
                sc[T * e : T * e + T, :K] = lax.dot_general(
                    x[i * EB + e], c, (((1,), (1,)), ((), ())), preferred_element_type=f32
                )
            rows = pl.ds(pl.multiple_of(i * EB, EB), EB)
            for g in range(T // 4):
                acc = sc[pl.ds(4 * g, EB, stride=T), :]
                for j in range(1, 4):
                    v = pltpu.roll(sc[pl.ds(4 * g + j, EB, stride=T), :], K * j, 1)
                    acc = jnp.where(lane == j, v, acc)
                flat[rows, 128 * g : 128 * g + 128] = acc.astype(bf)
            for j in range(8):
                at = pl.ds(pl.multiple_of(perm[j] * 256, 256), 256)
                flatp[rows, 256 * j : 256 * j + 256] = flat[rows, at]

        for j in range(H // 256):
            at = slice(256 * j, 256 * j + 256)
            hidden[:, at] = jnp.dot(flat[...], w[:, at], preferred_element_type=f32).astype(bf)

    scratch = [pltpu.VMEM((EB * T, 128), f32), pltpu.VMEM((n, T * K), bf)]
    return call(chain, body, "field", [shape(n, T * K), shape(n, H)], scratch, [tbl, perm], [comp, x, w])


def spread(df, rows, sc, tail=None):
    lane = lax.broadcasted_iota(jnp.int32, (EB, 128), 1)
    for g in range(T // 4):
        v = df[rows, 128 * g : 128 * g + 128].astype(f32)
        for j in range(4):
            w = v if j == 0 else pltpu.roll(v, 128 - K * j, 1)
            if tail is not None:
                w = jnp.where(lane < K, w, tail[4 * g + j : 4 * g + j + 1, :])
            sc[pl.ds(4 * g + j, EB, stride=T), :] = w


def silu_grad(value):
    sig = jax.nn.sigmoid(value)
    return sig * (1.0 + value * (1.0 - sig))


def grad_compress(chain, x, pre, up, bias, w, tbl, blk):
    n = tbl.shape[0]

    def body(tbl, blk, pre, up, bias, x, w, gpre, df, out, sc):
        @pl.loop(0, n // EB)
        def _(i):
            rows = pl.ds(pl.multiple_of(i * EB, EB), EB)
            u = up[pl.ds(pl.multiple_of((blk[0] + i) * EB, EB), EB), :].astype(f32)
            gpre[rows, :] = (u * silu_grad(pre[rows, :].astype(f32) + bias[...])).astype(bf)

        for j in range(T * K // 256):
            at = slice(256 * j, 256 * j + 256)
            df[:, at] = lax.dot_general(
                gpre[...], w[at, :], (((1,), (1,)), ((), ())), preferred_element_type=f32
            ).astype(bf)

        @pl.loop(0, n // EB)
        def _(i):
            spread(df, pl.ds(pl.multiple_of(i * EB, EB), EB), sc)
            for e in range(EB):
                s = sc[T * e : T * e + T, :K].astype(bf)
                r = lax.dot_general(s, x[i * EB + e], (((0,), (0,)), ((), ())), preferred_element_type=f32)
                out[tbl[i * EB + e]] = r.astype(bf)

    outs = [shape(n, H), shape(n, T * K), shape(n, K, D)]
    scratch = [pltpu.VMEM((EB * T, 128), f32)]
    return call(chain, body, "grad_compress", outs, scratch, [tbl, blk], [pre, up, bias, x, w])


def grad_weight(chain, flats, gpres):
    m = T * K // 2

    def body(*refs):
        ins, (keep, send, sums) = refs[:-3], refs[-3:]
        flats, gpres = ins[: len(ins) // 2], ins[len(ins) // 2 :]
        g = jnp.concatenate([r[...] for r in gpres], axis=0)
        for j in range(8):
            f = jnp.concatenate([r[:, 256 * j : 256 * j + 256] for r in flats], axis=0)
            r = lax.dot_general(f, g, (((0,), (0,)), ((), ())), preferred_element_type=f32).astype(bf)
            out, at = (keep, 256 * j) if j < 4 else (send, 256 * j - m)
            out[at : at + 256, :] = r
        sums[...] = jnp.zeros_like(sums)
        total = jnp.sum(g.astype(f32), axis=0, keepdims=True)
        for j in range(H // 128):
            sums[K + j : K + j + 1, :] = total[:, 128 * j : 128 * j + 128]

    outs = [shape(m, H), shape(m, H), shape(K + H // 128, 128, dtype=f32)]
    return call(chain, body, "grad_weight", outs, [], [], [*flats, *gpres])


def grad_projection(chain, x, dcomp, sums, tbl):
    n = tbl.shape[0]

    def body(tbl, dcomp, x, sums, out):
        out[...] = sums[...]

        @pl.loop(0, n // EB)
        def _(i):
            acc = out[:K, :T]
            for e in range(EB):
                acc = acc + lax.dot_general(
                    dcomp[tbl[i * EB + e]], x[i * EB + e], (((1,), (1,)), ((), ())), preferred_element_type=f32
                )
            out[:K, :T] = acc

    return call(chain, body, "grad_projection", [shape(*sums.shape, dtype=f32)], [], [tbl], [dcomp, x, sums])[0]


def grad_tokens(chain, df, comp, dcomp, tail, gx, dims, tbl, blk):
    n = tbl.shape[0]
    far = [] if gx is None else [gx]

    def body(tbl, blk, df, comp, dcomp, tail, *rest):
        out, mark, ov, sem, sc = rest[len(far) :]
        mark[...] = jnp.zeros_like(mark)

        def copy(i):
            return pltpu.make_async_copy(ov.at[pl.ds(i * EB, EB)], out.at[pl.ds((blk[0] + i) * EB, EB)], sem.at[i])

        @pl.loop(0, n // EB)
        def _(i):
            spread(df, pl.ds(pl.multiple_of(i * EB, EB), EB), sc, tail)
            for e in range(EB):
                s = sc[T * e : T * e + T, : 2 * K].astype(bf)
                at = tbl[i * EB + e]
                w = jnp.concatenate([comp[at], dcomp[at]], axis=0)
                ov[i * EB + e] = jnp.dot(s, w, preferred_element_type=f32).astype(bf)
            copy(i).start()

        for i in range(n // EB):
            copy(i).wait()

    outs = [pltpu.HBM(dims, bf), shape(8, 128, dtype=f32)]
    scratch = [pltpu.VMEM((n, T, D), bf), pltpu.SemaphoreType.DMA((n // EB,)), pltpu.VMEM((EB * T, 128), f32)]
    alias = {6: 0} if far else None
    return call(chain, body, "grad_tokens", outs, scratch, [tbl, blk], [df, comp, dcomp, tail], far, alias)[0]


def add_rows(chain, a, b, cut=False, dtype=bf):
    n, rest = a.shape[0], a.shape[1:]
    m = n // 2 if cut else n
    step = 10 if len(rest) == 2 else 16 if a.dtype == bf else 8

    def body(a, b, *outs):
        for k, out in enumerate(outs):

            @pl.loop(0, m // step)
            def _(i):
                to = pl.multiple_of(i * step, step)
                at = pl.ds(pl.multiple_of(k * m + i * step, step), step)
                out[pl.ds(to, step)] = (a[at].astype(f32) + b[at].astype(f32)).astype(out.dtype)

    outs = call(chain, body, "add", [shape(m, *rest, dtype=dtype)] * (n // m), [], [], [a, b])
    return outs if cut else outs[0]


def join_rows(chain, a, b):
    n, rest = a.shape[0], a.shape[1:]

    def body(a, b, out):
        @pl.loop(0, n // 10)
        def _(i):
            out[pl.ds(i * 10, 10)] = a[pl.ds(i * 10, 10)]
            out[pl.ds(n + i * 10, 10)] = b[pl.ds(i * 10, 10)]

    return call(chain, body, "join", [shape(2 * n, *rest)], [], [], [a, b])[0]


def tok_bits(i):
    x = i // 4
    g = x ^ (x >> 1)
    return {"A": g & 1, "B": g >> 1, "Z": (i >> 1) & 1}


def tok_flip(i, d):
    x = i // 4
    return {"A": (x ^ 1) * 4 + i % 4, "B": (3 - x) * 4 + i % 4, "Z": i ^ 2, "C": i ^ 1}[d]


def dp_bits(i):
    y = i // 2
    g = y ^ (y >> 1)
    return {"A": g & 1, "B": g >> 1, "Z": i & 1}


def dp_flip(i, d):
    y = i // 2
    return {"A": (y ^ 1) * 2 + i % 2, "B": (3 - y) * 2 + i % 2, "Z": i ^ 1}[d]


def place(bits, order):
    return bits[order[0]] * 4 + bits[order[1]] * 2 + bits[order[2]]


def tok_swap(x, step, orders):
    if step == "C":
        pairs = [(i, tok_flip(i, "C")) for i in range(16)]
    else:
        pairs = [(i, tok_flip(i, orders[i & 1][step])) for i in range(16)]
    return lax.ppermute(x, "tok", pairs)


def dp_swap(x, step):
    pairs = []
    for d in range(8):
        for t in range(16):
            pairs.append((d * 16 + t, dp_flip(d, DP_ORDERS[t & 1][step]) * 16 + t))
    return lax.ppermute(x, ("dp", "tok"), pairs)


def per_device(embeddings, projection, mlp_weight, mlp_bias, upstream):
    half = embeddings.shape[0] // NCH // 2
    part = half // 8
    tok = lax.axis_index("tok")
    core = tok & 1
    bits, dbits = tok_bits(tok), dp_bits(lax.axis_index("dp"))
    own = jnp.where(core == 0, place(dbits, DP_ORDERS[0]), place(dbits, DP_ORDERS[1]))
    owners = []
    for order in DP_ORDERS:
        table = [0] * 8
        for d in range(8):
            table[place(dp_bits(d), order)] = d
        owners.append(table)
    owners = jnp.asarray(owners, jnp.int32)[core]
    perm = owners[own ^ jnp.arange(8)].astype(jnp.int32)

    pt = jnp.tile(projection.T, (4, 4))
    same = (jnp.arange(4 * K)[:, None] // K) == (jnp.arange(4 * T)[None] // T)
    pt4 = jnp.where(same, pt, 0).astype(bf)
    tail = jnp.pad(projection.astype(f32), ((0, 0), (K, 128 - 2 * K)))
    bias = mlp_bias.reshape(1, H)

    e = jnp.arange(half, dtype=jnp.int32)
    tables, blocks = [], []
    for c in range(NCH):
        tabs = [((e // part) ^ place(bits, ORDERS[c][h])) * part + e % part for h in range(2)]
        tables.append((jnp.where(core == 0, tabs[0], tabs[1]), jnp.where(core == 0, tabs[1], tabs[0])))
        first = c * 2 * half // EB
        blocks.append(((first + core * (half // EB)).reshape(1), (first + (1 - core) * (half // EB)).reshape(1)))

    chain = Chain()
    chain.last = [perm, tail, bias, *(a for c in range(NCH) for pair in (tables[c], blocks[c]) for a in pair)]
    done = {}

    def total(swap, mine, got):
        for step in range(3):
            mine, send = add_rows(chain, mine, got, True)
            got = swap(send, step)
            yield
        mine = add_rows(chain, mine, got)
        for step in (2, 1, 0):
            got = swap(mine, step)
            yield
            mine = join_rows(chain, mine, got)
        return mine

    def chunk(c):
        tbl, blk = tables[c], blocks[c]

        def swap(x, step):
            return tok_swap(x, step, ORDERS[c])

        x1, other = compress(chain, embeddings, pt4, tbl[1], blk[1])
        got = swap(other, "C")
        yield
        x0, mine = compress(chain, embeddings, pt4, tbl[0], blk[0])
        yield
        mine = yield from total(swap, mine, got)
        other = swap(mine, "C")
        comp = (mine, other)
        yield
        f0, h0 = field(chain, x0, mine, mlp_weight, tbl[0], perm)
        yield
        f1, h1 = field(chain, x1, other, mlp_weight, tbl[1], perm)
        got = swap(h1, "C")
        yield
        pre = h0
        for step in range(3):
            pre = add_rows(chain, pre, got)
            got = swap(pre, step)
            yield
        pre = add_rows(chain, pre, got)
        got = swap(pre, "C")
        yield
        g1, d1, other = grad_compress(chain, x1, got, upstream, bias, mlp_weight, tbl[1], blk[1])
        got = swap(other, "C")
        yield
        g0, d0, mine = grad_compress(chain, x0, pre, upstream, bias, mlp_weight, tbl[0], blk[0])
        done[c] = ((f0, f1), (g0, g1))
        yield
        mine = yield from total(swap, mine, got)
        other = swap(mine, "C")
        dcomp = (mine, other)
        yield
        done["sums"] = grad_projection(chain, x0, mine, done["sums"], tbl[0])
        yield
        done["sums"] = grad_projection(chain, x1, other, done["sums"], tbl[1])
        yield
        for h, d in ((0, d0), (1, d1)):
            done["gx"] = grad_tokens(
                chain, d, comp[h], dcomp[h], tail, done.get("gx"), embeddings.shape, tbl[h], blk[h]
            )
            yield

    def weight():
        flats = [f for c in range(NCH) for f in done[c][0]]
        gpres = [g for c in range(NCH) for g in done[c][1]]
        keep, send, done["sums"] = grad_weight(chain, flats, gpres)
        got = dp_swap(send, 0)
        yield
        for step in (1, 2):
            keep, send = add_rows(chain, keep, got, True)
            got = dp_swap(send, step)
            yield
        done["w"] = add_rows(chain, keep, got, dtype=f32)
        yield

    def sums():
        x = done["sums"]
        for step in range(3):
            got = dp_swap(x, step)
            yield
            x = add_rows(chain, x, got, dtype=f32)
        done["sums"] = x
        yield

    steps = {c: chunk(c) for c in range(NCH)}
    steps["w"], steps["s"] = weight(), sums()
    for who in ORDER:
        next(steps[who])
    grad_p = done["sums"][:K, :T].T
    grad_b = done["sums"][K:].reshape(H)
    return done["gx"], done["w"], grad_p, grad_b


def solution(mesh):
    in_specs = (P("dp", "tok", None), P("tok", None), P("tok", None), P(), P("dp", None))
    out_specs = (P("dp", "tok", None), P(("tok", "dp"), None), P("tok", None), P())
    return jax.shard_map(
        per_device, mesh=mesh, in_specs=in_specs, out_specs=out_specs, check_vma=False
    )
```

```python
import jax
import jax.numpy as jnp
from jax import lax
from jax.experimental import pallas as pl
from jax.experimental.pallas import tpu as pltpu
from jax.sharding import PartitionSpec as P

f32 = jnp.float32
bf = jnp.bfloat16
T, K, D, H = 64, 32, 256, 1024
EB = 16
PITCH = T + 1
NCH = 2
ORDERS = (("ABZ", "BAZ"), ("ABZ", "BAZ"))
DP_ORDERS = ("ABZ", "BAZ")
ORDER = (
    0, 0, 0, 1, 1, 1, 0, 1, 0, 1, 0, 1, 0, 1, 0, 1, 0, 0, 0, 1,
    0, 1, 1, 0, 1, 0, 1, 0, 1, 0, 0, 1, 0, 1, 1, 1, "w", 0, 1, 0,
    1, 0, 1, 0, "w", 1, 0, 1, 0, 0, "w", 0, 1, 0, 1, 1, "s", 1, "w", "s",
    0, "s", 1, "s",
)


class Chain:
    def __init__(self):
        self.last = []


def call(chain, body, name, outs, scratch, smem=(), vmem=(), far=(), alias=None):
    specs = [pl.BlockSpec(memory_space=pltpu.SMEM)] * len(smem)
    specs += [pl.BlockSpec(memory_space=pltpu.VMEM)] * len(vmem)
    specs += [pl.BlockSpec(memory_space=pl.ANY)] * (len(far) + len(chain.last))
    vmem = [pltpu.with_memory_space_constraint(a, pltpu.VMEM) if a.size > 100000 else a for a in vmem]
    far = [pltpu.with_memory_space_constraint(a, pltpu.HBM) for a in far]
    ins, skip = len(smem) + len(vmem) + len(far), len(chain.last)

    def run(*refs):
        body(*refs[:ins], *refs[ins + skip :])

    def place(out):
        return pl.BlockSpec(memory_space=pltpu.VMEM if isinstance(out, jax.ShapeDtypeStruct) else pl.ANY)

    result = pl.pallas_call(
        run,
        out_shape=outs,
        in_specs=specs,
        out_specs=[place(out) for out in outs],
        scratch_shapes=scratch,
        input_output_aliases=alias or {},
        compiler_params=pltpu.CompilerParams(vmem_limit_bytes=8 * 1024 * 1024),
        cost_estimate=pl.CostEstimate(flops=int(2e10), bytes_accessed=1000, transcendentals=0),
        name=name,
    )(*smem, *vmem, *far, *chain.last)
    chain.last = [result[-1]]
    return result


def shape(*dims, dtype=bf):
    return jax.ShapeDtypeStruct(dims, dtype)


def compress(chain, x, pt4, tbl, blk):
    n = tbl.shape[0]

    def body(tbl, blk, pt4, x, xv, out, sem):
        def copy(i):
            return pltpu.make_async_copy(x.at[pl.ds((blk[0] + i) * EB, EB)], xv.at[pl.ds(i * EB, EB)], sem.at[i])

        for i in range(n // EB):
            copy(i).start()

        @pl.loop(0, n // EB)
        def _(i):
            copy(i).wait()
            for g in range(EB // 4):
                x4 = xv[pl.ds(i * EB + 4 * g, 4)].reshape(4 * T, D)
                r = jnp.dot(pt4[...], x4, preferred_element_type=f32).astype(bf)
                for j in range(4):
                    out[tbl[i * EB + 4 * g + j]] = r[K * j : K * j + K]

    outs = [shape(n, T, D), shape(n, K, D)]
    return call(chain, body, "compress", outs, [pltpu.SemaphoreType.DMA((n // EB,))], [tbl, blk], [pt4], [x])


def field(chain, x, comp, w, tbl, perm):
    n = tbl.shape[0]

    def body(tbl, perm, comp, x, w, flatp, hidden, sc, flat):
        lane = lax.broadcasted_iota(jnp.int32, (EB, 128), 1) // K

        @pl.loop(0, n // EB)
        def _(i):
            for e in range(EB):
                c = comp[tbl[i * EB + e]]
                sc[PITCH * e : PITCH * e + T, :K] = lax.dot_general(
                    x[i * EB + e], c, (((1,), (1,)), ((), ())), preferred_element_type=f32
                )
            rows = pl.ds(pl.multiple_of(i * EB, EB), EB)
            for g in range(T // 4):
                acc = sc[pl.ds(4 * g, EB, stride=PITCH), :]
                for j in range(1, 4):
                    v = pltpu.roll(sc[pl.ds(4 * g + j, EB, stride=PITCH), :], K * j, 1)
                    acc = jnp.where(lane == j, v, acc)
                flat[rows, 128 * g : 128 * g + 128] = acc.astype(bf)
            for j in range(8):
                at = pl.ds(pl.multiple_of(perm[j] * 256, 256), 256)
                flatp[rows, 256 * j : 256 * j + 256] = flat[rows, at]

        for j in range(H // 256):
            at = slice(256 * j, 256 * j + 256)
            hidden[:, at] = jnp.dot(flat[...], w[:, at], preferred_element_type=f32).astype(bf)

    scratch = [pltpu.VMEM((EB * PITCH, 128), f32), pltpu.VMEM((n, T * K), bf)]
    return call(chain, body, "field", [shape(n, T * K), shape(n, H)], scratch, [tbl, perm], [comp, x, w])


def spread(df, rows, sc, tail=None):
    lane = lax.broadcasted_iota(jnp.int32, (EB, 128), 1)
    for g in range(T // 4):
        v = df[rows, 128 * g : 128 * g + 128].astype(f32)
        for j in range(4):
            w = v if j == 0 else pltpu.roll(v, 128 - K * j, 1)
            if tail is not None:
                w = jnp.where(lane < K, w, tail[4 * g + j : 4 * g + j + 1, :])
            sc[pl.ds(4 * g + j, EB, stride=PITCH), :] = w


def silu_grad(value):
    sig = jax.nn.sigmoid(value)
    return sig * (1.0 + value * (1.0 - sig))


def grad_compress(chain, x, pre, up, bias, w, tbl, blk):
    n = tbl.shape[0]

    def body(tbl, blk, pre, up, bias, x, w, gpre, df, out, sc):
        @pl.loop(0, n // EB)
        def _(i):
            rows = pl.ds(pl.multiple_of(i * EB, EB), EB)
            u = up[pl.ds(pl.multiple_of((blk[0] + i) * EB, EB), EB), :].astype(f32)
            gpre[rows, :] = (u * silu_grad(pre[rows, :].astype(f32) + bias[...])).astype(bf)

        for j in range(T * K // 256):
            at = slice(256 * j, 256 * j + 256)
            df[:, at] = lax.dot_general(
                gpre[...], w[at, :], (((1,), (1,)), ((), ())), preferred_element_type=f32
            ).astype(bf)

        @pl.loop(0, n // EB)
        def _(i):
            spread(df, pl.ds(pl.multiple_of(i * EB, EB), EB), sc)
            for e in range(EB):
                s = sc[PITCH * e : PITCH * e + T, :K].astype(bf)
                r = lax.dot_general(s, x[i * EB + e], (((0,), (0,)), ((), ())), preferred_element_type=f32)
                out[tbl[i * EB + e]] = r.astype(bf)

    outs = [shape(n, H), shape(n, T * K), shape(n, K, D)]
    scratch = [pltpu.VMEM((EB * PITCH, 128), f32)]
    return call(chain, body, "grad_compress", outs, scratch, [tbl, blk], [pre, up, bias, x, w])


def grad_weight(chain, flats, gpres):
    m = T * K // 2

    def body(*refs):
        ins, (keep, send, sums) = refs[:-3], refs[-3:]
        flats, gpres = ins[: len(ins) // 2], ins[len(ins) // 2 :]
        g = jnp.concatenate([r[...] for r in gpres], axis=0)
        for j in range(8):
            f = jnp.concatenate([r[:, 256 * j : 256 * j + 256] for r in flats], axis=0)
            r = lax.dot_general(f, g, (((0,), (0,)), ((), ())), preferred_element_type=f32).astype(bf)
            out, at = (keep, 256 * j) if j < 4 else (send, 256 * j - m)
            out[at : at + 256, :] = r
        sums[...] = jnp.zeros_like(sums)
        total = jnp.sum(g.astype(f32), axis=0, keepdims=True)
        for j in range(H // 128):
            sums[K + j : K + j + 1, :] = total[:, 128 * j : 128 * j + 128]

    outs = [shape(m, H), shape(m, H), shape(K + H // 128, 128, dtype=f32)]
    return call(chain, body, "grad_weight", outs, [], [], [*flats, *gpres])


def grad_projection(chain, x, dcomp, sums, tbl):
    n = tbl.shape[0]

    def body(tbl, dcomp, x, sums, out):
        out[...] = sums[...]

        @pl.loop(0, n // EB)
        def _(i):
            acc = out[:K, :T]
            for e in range(EB):
                acc = acc + lax.dot_general(
                    dcomp[tbl[i * EB + e]], x[i * EB + e], (((1,), (1,)), ((), ())), preferred_element_type=f32
                )
            out[:K, :T] = acc

    return call(chain, body, "grad_projection", [shape(*sums.shape, dtype=f32)], [], [tbl], [dcomp, x, sums])[0]


def grad_tokens(chain, df, comp, dcomp, tail, gx, dims, tbl, blk):
    n = tbl.shape[0]
    far = [] if gx is None else [gx]

    def body(tbl, blk, df, comp, dcomp, tail, *rest):
        out, mark, ov, sem, sc = rest[len(far) :]
        mark[...] = jnp.zeros_like(mark)

        def copy(i):
            return pltpu.make_async_copy(ov.at[pl.ds(i * EB, EB)], out.at[pl.ds((blk[0] + i) * EB, EB)], sem.at[i])

        @pl.loop(0, n // EB)
        def _(i):
            spread(df, pl.ds(pl.multiple_of(i * EB, EB), EB), sc, tail)
            for e in range(EB):
                s = sc[PITCH * e : PITCH * e + T, : 2 * K].astype(bf)
                at = tbl[i * EB + e]
                w = jnp.concatenate([comp[at], dcomp[at]], axis=0)
                ov[i * EB + e] = jnp.dot(s, w, preferred_element_type=f32).astype(bf)
            copy(i).start()

        for i in range(n // EB):
            copy(i).wait()

    outs = [pltpu.HBM(dims, bf), shape(8, 128, dtype=f32)]
    scratch = [pltpu.VMEM((n, T, D), bf), pltpu.SemaphoreType.DMA((n // EB,)), pltpu.VMEM((EB * PITCH, 128), f32)]
    alias = {6: 0} if far else None
    return call(chain, body, "grad_tokens", outs, scratch, [tbl, blk], [df, comp, dcomp, tail], far, alias)[0]


def add_rows(chain, a, b, cut=False, dtype=bf):
    n, rest = a.shape[0], a.shape[1:]
    m = n // 2 if cut else n
    step = 10 if len(rest) == 2 else 16 if a.dtype == bf else 8

    def body(a, b, *outs):
        for k, out in enumerate(outs):

            @pl.loop(0, m // step)
            def _(i):
                to = pl.multiple_of(i * step, step)
                at = pl.ds(pl.multiple_of(k * m + i * step, step), step)
                out[pl.ds(to, step)] = (a[at].astype(f32) + b[at].astype(f32)).astype(out.dtype)

    outs = call(chain, body, "add", [shape(m, *rest, dtype=dtype)] * (n // m), [], [], [a, b])
    return outs if cut else outs[0]


def split_sums(chain, a, b):
    def body(a, b, gp, gb):
        gp[...] = (a[:K, :T] + b[:K, :T]).T
        gb[...] = a[K:, :] + b[K:, :]

    outs = [shape(T, K, dtype=f32), shape(H // 128, 128, dtype=f32)]
    return call(chain, body, "add", outs, [], [], [a, b])


def join_rows(chain, a, b):
    n, rest = a.shape[0], a.shape[1:]

    def body(a, b, out):
        @pl.loop(0, n // 10)
        def _(i):
            out[pl.ds(i * 10, 10)] = a[pl.ds(i * 10, 10)]
            out[pl.ds(n + i * 10, 10)] = b[pl.ds(i * 10, 10)]

    return call(chain, body, "join", [shape(2 * n, *rest)], [], [], [a, b])[0]


def tok_bits(i):
    x = i // 4
    g = x ^ (x >> 1)
    return {"A": g & 1, "B": g >> 1, "Z": (i >> 1) & 1}


def tok_flip(i, d):
    x = i // 4
    return {"A": (x ^ 1) * 4 + i % 4, "B": (3 - x) * 4 + i % 4, "Z": i ^ 2, "C": i ^ 1}[d]


def dp_bits(i):
    y = i // 2
    g = y ^ (y >> 1)
    return {"A": g & 1, "B": g >> 1, "Z": i & 1}


def dp_flip(i, d):
    y = i // 2
    return {"A": (y ^ 1) * 2 + i % 2, "B": (3 - y) * 2 + i % 2, "Z": i ^ 1}[d]


def place(bits, order):
    return bits[order[0]] * 4 + bits[order[1]] * 2 + bits[order[2]]


def tok_swap(x, step, orders):
    if step == "C":
        pairs = [(i, tok_flip(i, "C")) for i in range(16)]
    else:
        pairs = [(i, tok_flip(i, orders[i & 1][step])) for i in range(16)]
    return lax.ppermute(x, "tok", pairs)


def dp_swap(x, step):
    pairs = []
    for d in range(8):
        for t in range(16):
            pairs.append((d * 16 + t, dp_flip(d, DP_ORDERS[t & 1][step]) * 16 + t))
    return lax.ppermute(x, ("dp", "tok"), pairs)


def per_device(embeddings, projection, mlp_weight, mlp_bias, upstream):
    half = embeddings.shape[0] // NCH // 2
    part = half // 8
    tok = lax.axis_index("tok")
    core = tok & 1
    bits, dbits = tok_bits(tok), dp_bits(lax.axis_index("dp"))
    own = jnp.where(core == 0, place(dbits, DP_ORDERS[0]), place(dbits, DP_ORDERS[1])) ^ jnp.arange(8, dtype=jnp.int32)
    digits = (own >> 2, (own >> 1) & 1, own & 1)
    blocks = []
    for order in DP_ORDERS:
        at = dict(zip(order, digits))
        g = at["A"] + 2 * at["B"]
        blocks.append((g ^ (g >> 1)) * 2 + at["Z"])
    perm = jnp.where(core == 0, blocks[0], blocks[1])

    pt4 = sum(
        jnp.pad(projection.T.astype(f32), ((K * j, 3 * K - K * j), (T * j, 3 * T - T * j))) for j in range(4)
    ).astype(bf)
    tail = jnp.pad(projection.astype(f32), ((0, 0), (K, 128 - 2 * K)))
    bias = mlp_bias.reshape(1, H)

    e = jnp.arange(half, dtype=jnp.int32)
    tables, blocks = [], []
    for c in range(NCH):
        tabs = [((e // part) ^ place(bits, ORDERS[c][h])) * part + e % part for h in range(2)]
        tables.append((jnp.where(core == 0, tabs[0], tabs[1]), jnp.where(core == 0, tabs[1], tabs[0])))
        first = c * 2 * half // EB
        blocks.append(((first + core * (half // EB)).reshape(1), (first + (1 - core) * (half // EB)).reshape(1)))

    chain = Chain()
    chain.last = [perm, tail, bias, *(a for c in range(NCH) for pair in (tables[c], blocks[c]) for a in pair)]
    done = {}

    def total(swap, mine, got):
        for step in range(3):
            mine, send = add_rows(chain, mine, got, True)
            got = swap(send, step)
            yield
        mine = add_rows(chain, mine, got)
        for step in (2, 1, 0):
            got = swap(mine, step)
            yield
            mine = join_rows(chain, mine, got)
        return mine

    def chunk(c):
        tbl, blk = tables[c], blocks[c]

        def swap(x, step):
            return tok_swap(x, step, ORDERS[c])

        x1, other = compress(chain, embeddings, pt4, tbl[1], blk[1])
        got = swap(other, "C")
        yield
        x0, mine = compress(chain, embeddings, pt4, tbl[0], blk[0])
        yield
        mine = yield from total(swap, mine, got)
        other = swap(mine, "C")
        comp = (mine, other)
        yield
        f0, h0 = field(chain, x0, mine, mlp_weight, tbl[0], perm)
        yield
        f1, h1 = field(chain, x1, other, mlp_weight, tbl[1], perm)
        got = swap(h1, "C")
        yield
        pre = h0
        for step in range(3):
            pre = add_rows(chain, pre, got)
            got = swap(pre, step)
            yield
        pre = add_rows(chain, pre, got)
        got = swap(pre, "C")
        yield
        g1, d1, other = grad_compress(chain, x1, got, upstream, bias, mlp_weight, tbl[1], blk[1])
        got = swap(other, "C")
        yield
        g0, d0, mine = grad_compress(chain, x0, pre, upstream, bias, mlp_weight, tbl[0], blk[0])
        done[c] = ((f0, f1), (g0, g1))
        yield
        mine = yield from total(swap, mine, got)
        other = swap(mine, "C")
        dcomp = (mine, other)
        yield
        done["sums"] = grad_projection(chain, x0, mine, done["sums"], tbl[0])
        yield
        done["sums"] = grad_projection(chain, x1, other, done["sums"], tbl[1])
        yield
        for h, d in ((0, d0), (1, d1)):
            done["gx"] = grad_tokens(
                chain, d, comp[h], dcomp[h], tail, done.get("gx"), embeddings.shape, tbl[h], blk[h]
            )
            yield

    def weight():
        flats = [f for c in range(NCH) for f in done[c][0]]
        gpres = [g for c in range(NCH) for g in done[c][1]]
        keep, send, done["sums"] = grad_weight(chain, flats, gpres)
        got = dp_swap(send, 0)
        yield
        for step in (1, 2):
            keep, send = add_rows(chain, keep, got, True)
            got = dp_swap(send, step)
            yield
        done["w"] = add_rows(chain, keep, got, dtype=f32)
        yield

    def sums():
        x = done["sums"]
        for step in range(3):
            got = dp_swap(x, step)
            yield
            if step < 2:
                x = add_rows(chain, x, got, dtype=f32)
        done["sums"] = split_sums(chain, x, got)
        yield

    steps = {c: chunk(c) for c in range(NCH)}
    steps["w"], steps["s"] = weight(), sums()
    for who in ORDER:
        next(steps[who])
    grad_p, grad_b = done["sums"]
    return done["gx"], done["w"], grad_p, grad_b.reshape(H)


def solution(mesh):
    in_specs = (P("dp", "tok", None), P("tok", None), P("tok", None), P(), P("dp", None))
    out_specs = (P("dp", "tok", None), P(("tok", "dp"), None), P("tok", None), P())
    return jax.shard_map(
        per_device, mesh=mesh, in_specs=in_specs, out_specs=out_specs, check_vma=False
    )
```

```python
import jax
import jax.numpy as jnp
from jax import lax
from jax.experimental import pallas as pl
from jax.experimental.pallas import tpu as pltpu
from jax.sharding import PartitionSpec as P

f32 = jnp.float32
bf = jnp.bfloat16
T, K, D, H = 64, 32, 256, 1024
EB = 16
PITCH = T + 1
NCH = 2
ORDERS = (("AZB", "BZA"), ("AZB", "BZA"))
DP_ORDERS = ("ABZ", "BAZ")
ORDER = (
    0, 0, 0, 1, 1, 1, 0, 1, 0, 1, 0, 1, 0, 1, 0, 1, 0, 0, 0, 1,
    0, 1, 1, 0, 1, 0, 1, 0, 1, 0, 0, 1, 0, 1, 1, 1, "w", 0, 1, 0,
    1, 0, 1, 0, "w", 1, 0, 1, 0, 0, "w", 0, 1, 0, 1, 1, "s", 1, "w", "s",
    0, "s", 1, "s",
)


class Chain:
    def __init__(self):
        self.last = []


def call(chain, body, name, outs, scratch, smem=(), vmem=(), far=(), alias=None):
    specs = [pl.BlockSpec(memory_space=pltpu.SMEM)] * len(smem)
    specs += [pl.BlockSpec(memory_space=pltpu.VMEM)] * len(vmem)
    specs += [pl.BlockSpec(memory_space=pl.ANY)] * (len(far) + len(chain.last))
    vmem = [pltpu.with_memory_space_constraint(a, pltpu.VMEM) if a.size > 100000 else a for a in vmem]
    far = [pltpu.with_memory_space_constraint(a, pltpu.HBM) for a in far]
    ins, skip = len(smem) + len(vmem) + len(far), len(chain.last)

    def run(*refs):
        body(*refs[:ins], *refs[ins + skip :])

    def place(out):
        return pl.BlockSpec(memory_space=pltpu.VMEM if isinstance(out, jax.ShapeDtypeStruct) else pl.ANY)

    result = pl.pallas_call(
        run,
        out_shape=outs,
        in_specs=specs,
        out_specs=[place(out) for out in outs],
        scratch_shapes=scratch,
        input_output_aliases=alias or {},
        compiler_params=pltpu.CompilerParams(vmem_limit_bytes=8 * 1024 * 1024),
        cost_estimate=pl.CostEstimate(flops=int(2e10), bytes_accessed=1000, transcendentals=0),
        name=name,
    )(*smem, *vmem, *far, *chain.last)
    chain.last = [result[-1]]
    return result


def shape(*dims, dtype=bf):
    return jax.ShapeDtypeStruct(dims, dtype)


def compress(chain, x, pt, tbl, blk):
    n = tbl.shape[0]

    def body(tbl, blk, pt, x, xv, out, sem, pt4):
        def copy(i):
            return pltpu.make_async_copy(x.at[pl.ds((blk[0] + i) * EB, EB)], xv.at[pl.ds(i * EB, EB)], sem.at[i])

        for i in range(n // EB):
            copy(i).start()

        wide = jnp.concatenate([pt[...].astype(f32)] * 4, axis=1)
        lane = lax.broadcasted_iota(jnp.int32, (K, 4 * T), 1) // T
        for j in range(4):
            pt4[K * j : K * j + K, :] = jnp.where(lane == j, wide, 0.0).astype(bf)

        @pl.loop(0, n // EB)
        def _(i):
            copy(i).wait()
            for g in range(EB // 4):
                x4 = xv[pl.ds(i * EB + 4 * g, 4)].reshape(4 * T, D)
                r = jnp.dot(pt4[...], x4, preferred_element_type=f32).astype(bf)
                for j in range(4):
                    out[tbl[i * EB + 4 * g + j]] = r[K * j : K * j + K]

    outs = [shape(n, T, D), shape(n, K, D)]
    scratch = [pltpu.SemaphoreType.DMA((n // EB,)), pltpu.VMEM((4 * K, 4 * T), bf)]
    return call(chain, body, "compress", outs, scratch, [tbl, blk], [pt], [x])


def field(chain, x, comp, w, tbl, perm):
    n = tbl.shape[0]

    def body(tbl, perm, comp, x, w, flatp, hidden, sc, flat):
        lane = lax.broadcasted_iota(jnp.int32, (EB, 128), 1) // K

        @pl.loop(0, n // EB)
        def _(i):
            for e in range(EB):
                c = comp[tbl[i * EB + e]]
                sc[PITCH * e : PITCH * e + T, :K] = lax.dot_general(
                    x[i * EB + e], c, (((1,), (1,)), ((), ())), preferred_element_type=f32
                )
            rows = pl.ds(pl.multiple_of(i * EB, EB), EB)
            for g in range(T // 4):
                acc = sc[pl.ds(4 * g, EB, stride=PITCH), :]
                for j in range(1, 4):
                    v = pltpu.roll(sc[pl.ds(4 * g + j, EB, stride=PITCH), :], K * j, 1)
                    acc = jnp.where(lane == j, v, acc)
                flat[rows, 128 * g : 128 * g + 128] = acc.astype(bf)
            for j in range(8):
                at = pl.ds(pl.multiple_of(perm[j] * 256, 256), 256)
                flatp[rows, 256 * j : 256 * j + 256] = flat[rows, at]

        for j in range(H // 256):
            at = slice(256 * j, 256 * j + 256)
            hidden[:, at] = jnp.dot(flat[...], w[:, at], preferred_element_type=f32).astype(bf)

    scratch = [pltpu.VMEM((EB * PITCH, 128), f32), pltpu.VMEM((n, T * K), bf)]
    return call(chain, body, "field", [shape(n, T * K), shape(n, H)], scratch, [tbl, perm], [comp, x, w])


def spread(df, rows, sc, tail=None):
    lane = lax.broadcasted_iota(jnp.int32, (EB, 128), 1)
    for g in range(T // 4):
        v = df[rows, 128 * g : 128 * g + 128].astype(f32)
        for j in range(4):
            w = v if j == 0 else pltpu.roll(v, 128 - K * j, 1)
            if tail is not None:
                w = jnp.where(lane < K, w, tail[4 * g + j : 4 * g + j + 1, :])
            sc[pl.ds(4 * g + j, EB, stride=PITCH), :] = w


def silu_grad(value):
    sig = jax.nn.sigmoid(value)
    return sig * (1.0 + value * (1.0 - sig))


def grad_compress(chain, x, pre, up, bias, w, tbl, blk):
    n = tbl.shape[0]

    def body(tbl, blk, pre, up, bias, x, w, gpre, df, out, sc):
        @pl.loop(0, n // EB)
        def _(i):
            rows = pl.ds(pl.multiple_of(i * EB, EB), EB)
            u = up[pl.ds(pl.multiple_of((blk[0] + i) * EB, EB), EB), :].astype(f32)
            gpre[rows, :] = (u * silu_grad(pre[rows, :].astype(f32) + bias[...])).astype(bf)

        for j in range(T * K // 256):
            at = slice(256 * j, 256 * j + 256)
            df[:, at] = lax.dot_general(
                gpre[...], w[at, :], (((1,), (1,)), ((), ())), preferred_element_type=f32
            ).astype(bf)

        @pl.loop(0, n // EB)
        def _(i):
            spread(df, pl.ds(pl.multiple_of(i * EB, EB), EB), sc)
            for e in range(EB):
                s = sc[PITCH * e : PITCH * e + T, :K].astype(bf)
                r = lax.dot_general(s, x[i * EB + e], (((0,), (0,)), ((), ())), preferred_element_type=f32)
                out[tbl[i * EB + e]] = r.astype(bf)

    outs = [shape(n, H), shape(n, T * K), shape(n, K, D)]
    scratch = [pltpu.VMEM((EB * PITCH, 128), f32)]
    return call(chain, body, "grad_compress", outs, scratch, [tbl, blk], [pre, up, bias, x, w])


def grad_weight(chain, flats, gpres):
    m = T * K // 2

    def body(*refs):
        ins, (keep, send, sums) = refs[:-3], refs[-3:]
        flats, gpres = ins[: len(ins) // 2], ins[len(ins) // 2 :]
        g = jnp.concatenate([r[...] for r in gpres], axis=0)
        for j in range(8):
            f = jnp.concatenate([r[:, 256 * j : 256 * j + 256] for r in flats], axis=0)
            r = lax.dot_general(f, g, (((0,), (0,)), ((), ())), preferred_element_type=f32).astype(bf)
            out, at = (keep, 256 * j) if j < 4 else (send, 256 * j - m)
            out[at : at + 256, :] = r
        sums[...] = jnp.zeros_like(sums)
        total = jnp.sum(g.astype(f32), axis=0, keepdims=True)
        for j in range(H // 128):
            sums[K + j : K + j + 1, :] = total[:, 128 * j : 128 * j + 128]

    outs = [shape(m, H), shape(m, H), shape(K + H // 128, 128, dtype=f32)]
    return call(chain, body, "grad_weight", outs, [], [], [*flats, *gpres])


def grad_projection(chain, x, dcomp, sums, tbl):
    n = tbl.shape[0]

    def body(tbl, dcomp, x, sums, out):
        out[...] = sums[...]

        @pl.loop(0, n // EB)
        def _(i):
            acc = out[:K, :T]
            for e in range(EB):
                acc = acc + lax.dot_general(
                    dcomp[tbl[i * EB + e]], x[i * EB + e], (((1,), (1,)), ((), ())), preferred_element_type=f32
                )
            out[:K, :T] = acc

    return call(chain, body, "grad_projection", [shape(*sums.shape, dtype=f32)], [], [tbl], [dcomp, x, sums])[0]


def grad_tokens(chain, df, comp, dcomp, pt, gx, dims, tbl, blk):
    n = tbl.shape[0]
    far = [] if gx is None else [gx]

    def body(tbl, blk, df, comp, dcomp, pt, *rest):
        out, mark, ov, sem, sc, tail = rest[len(far) :]
        p = pt[...].astype(f32).T
        tail[:, : 2 * K] = jnp.concatenate([p, p], axis=1)
        mark[...] = jnp.zeros_like(mark)

        def copy(i):
            return pltpu.make_async_copy(ov.at[pl.ds(i * EB, EB)], out.at[pl.ds((blk[0] + i) * EB, EB)], sem.at[i])

        @pl.loop(0, n // EB)
        def _(i):
            spread(df, pl.ds(pl.multiple_of(i * EB, EB), EB), sc, tail)
            for e in range(EB):
                s = sc[PITCH * e : PITCH * e + T, : 2 * K].astype(bf)
                at = tbl[i * EB + e]
                w = jnp.concatenate([comp[at], dcomp[at]], axis=0)
                ov[i * EB + e] = jnp.dot(s, w, preferred_element_type=f32).astype(bf)
            copy(i).start()

        for i in range(n // EB):
            copy(i).wait()

    outs = [pltpu.HBM(dims, bf), shape(8, 128, dtype=f32)]
    scratch = [pltpu.VMEM((n, T, D), bf), pltpu.SemaphoreType.DMA((n // EB,)), pltpu.VMEM((EB * PITCH, 128), f32)]
    scratch += [pltpu.VMEM((T, 128), f32)]
    alias = {6: 0} if far else None
    return call(chain, body, "grad_tokens", outs, scratch, [tbl, blk], [df, comp, dcomp, pt], far, alias)[0]


def add_rows(chain, a, b, cut=False, dtype=bf):
    n, rest = a.shape[0], a.shape[1:]
    m = n // 2 if cut else n
    step = 10 if len(rest) == 2 else 16 if a.dtype == bf else 8

    def body(a, b, *outs):
        for k, out in enumerate(outs):

            @pl.loop(0, m // step)
            def _(i):
                to = pl.multiple_of(i * step, step)
                at = pl.ds(pl.multiple_of(k * m + i * step, step), step)
                out[pl.ds(to, step)] = (a[at].astype(f32) + b[at].astype(f32)).astype(out.dtype)

    outs = call(chain, body, "add", [shape(m, *rest, dtype=dtype)] * (n // m), [], [], [a, b])
    return outs if cut else outs[0]


def add_out(chain, a, b):
    n, m, step = a.shape[0], a.shape[1], 64

    def body(a, b, out, mark, ov, sem):
        mark[...] = jnp.zeros_like(mark)
        copies = []
        for i in range(n // step):
            at = pl.ds(i * step, step)
            ov[at] = a[at].astype(f32) + b[at].astype(f32)
            copies.append(pltpu.make_async_copy(ov.at[at], out.at[at], sem.at[i]))
            copies[-1].start()
        for copy in copies:
            copy.wait()

    outs = [pltpu.HBM((n, m), f32), shape(8, 128, dtype=f32)]
    scratch = [pltpu.VMEM((n, m), f32), pltpu.SemaphoreType.DMA((n // step,))]
    return call(chain, body, "add", outs, scratch, [], [a, b])[0]


def split_sums(chain, a, b):
    def body(a, b, gp, gb):
        gp[...] = a[:K, :T] + b[:K, :T]
        gb[...] = a[K:, :] + b[K:, :]

    outs = [shape(K, T, dtype=f32), shape(H // 128, 128, dtype=f32)]
    return call(chain, body, "add", outs, [], [], [a, b])


def join_rows(chain, a, b):
    n, rest = a.shape[0], a.shape[1:]

    def body(a, b, out):
        @pl.loop(0, n // 10)
        def _(i):
            out[pl.ds(i * 10, 10)] = a[pl.ds(i * 10, 10)]
            out[pl.ds(n + i * 10, 10)] = b[pl.ds(i * 10, 10)]

    return call(chain, body, "join", [shape(2 * n, *rest)], [], [], [a, b])[0]


def tok_bits(i):
    x = i // 4
    g = x ^ (x >> 1)
    return {"A": g & 1, "B": g >> 1, "Z": (i >> 1) & 1}


def tok_flip(i, d):
    x = i // 4
    return {"A": (x ^ 1) * 4 + i % 4, "B": (3 - x) * 4 + i % 4, "Z": i ^ 2, "C": i ^ 1}[d]


def dp_bits(i):
    y = i // 2
    g = y ^ (y >> 1)
    return {"A": g & 1, "B": g >> 1, "Z": i & 1}


def dp_flip(i, d):
    y = i // 2
    return {"A": (y ^ 1) * 2 + i % 2, "B": (3 - y) * 2 + i % 2, "Z": i ^ 1}[d]


def place(bits, order):
    return bits[order[0]] * 4 + bits[order[1]] * 2 + bits[order[2]]


def tok_swap(x, step, orders):
    if step == "C":
        pairs = [(i, tok_flip(i, "C")) for i in range(16)]
    else:
        pairs = [(i, tok_flip(i, orders[i & 1][step])) for i in range(16)]
    return lax.ppermute(x, "tok", pairs)


def dp_swap(x, step):
    pairs = []
    for d in range(8):
        for t in range(16):
            pairs.append((d * 16 + t, dp_flip(d, DP_ORDERS[t & 1][step]) * 16 + t))
    return lax.ppermute(x, ("dp", "tok"), pairs)


def per_device(embeddings, projection, mlp_weight, mlp_bias, upstream):
    half = embeddings.shape[0] // NCH // 2
    part = half // 8
    tok = lax.axis_index("tok")
    core = tok & 1
    bits, dbits = tok_bits(tok), dp_bits(lax.axis_index("dp"))
    own = jnp.where(core == 0, place(dbits, DP_ORDERS[0]), place(dbits, DP_ORDERS[1])) ^ jnp.arange(8, dtype=jnp.int32)
    digits = (own >> 2, (own >> 1) & 1, own & 1)
    blocks = []
    for order in DP_ORDERS:
        at = dict(zip(order, digits))
        g = at["A"] + 2 * at["B"]
        blocks.append((g ^ (g >> 1)) * 2 + at["Z"])
    perm = jnp.where(core == 0, blocks[0], blocks[1])

    pt = projection.T
    bias = mlp_bias.reshape(1, H)

    e = jnp.arange(half, dtype=jnp.int32)
    tables, blocks = [], []
    for c in range(NCH):
        tabs = [((e // part) ^ place(bits, ORDERS[c][h])) * part + e % part for h in range(2)]
        tables.append((jnp.where(core == 0, tabs[0], tabs[1]), jnp.where(core == 0, tabs[1], tabs[0])))
        first = c * 2 * half // EB
        blocks.append(((first + core * (half // EB)).reshape(1), (first + (1 - core) * (half // EB)).reshape(1)))

    chain = Chain()
    chain.last = [perm, bias, *(a for c in range(NCH) for pair in (tables[c], blocks[c]) for a in pair)]
    done = {}

    def total(swap, mine, got):
        for step in range(3):
            mine, send = add_rows(chain, mine, got, True)
            got = swap(send, step)
            yield
        mine = add_rows(chain, mine, got)
        for step in (2, 1, 0):
            got = swap(mine, step)
            yield
            mine = join_rows(chain, mine, got)
        return mine

    def chunk(c):
        tbl, blk = tables[c], blocks[c]

        def swap(x, step):
            return tok_swap(x, step, ORDERS[c])

        x1, other = compress(chain, embeddings, pt, tbl[1], blk[1])
        got = swap(other, "C")
        yield
        x0, mine = compress(chain, embeddings, pt, tbl[0], blk[0])
        yield
        mine = yield from total(swap, mine, got)
        other = swap(mine, "C")
        comp = (mine, other)
        yield
        f0, h0 = field(chain, x0, mine, mlp_weight, tbl[0], perm)
        yield
        f1, h1 = field(chain, x1, other, mlp_weight, tbl[1], perm)
        got = swap(h1, "C")
        yield
        pre = h0
        for step in range(3):
            pre = add_rows(chain, pre, got)
            got = swap(pre, step)
            yield
        pre = add_rows(chain, pre, got)
        got = swap(pre, "C")
        yield
        g1, d1, other = grad_compress(chain, x1, got, upstream, bias, mlp_weight, tbl[1], blk[1])
        got = swap(other, "C")
        yield
        g0, d0, mine = grad_compress(chain, x0, pre, upstream, bias, mlp_weight, tbl[0], blk[0])
        done[c] = ((f0, f1), (g0, g1))
        yield
        mine = yield from total(swap, mine, got)
        other = swap(mine, "C")
        dcomp = (mine, other)
        yield
        done["sums"] = grad_projection(chain, x0, mine, done["sums"], tbl[0])
        yield
        done["sums"] = grad_projection(chain, x1, other, done["sums"], tbl[1])
        yield
        for h, d in ((0, d0), (1, d1)):
            done["gx"] = grad_tokens(
                chain, d, comp[h], dcomp[h], pt, done.get("gx"), embeddings.shape, tbl[h], blk[h]
            )
            yield

    def weight():
        flats = [f for c in range(NCH) for f in done[c][0]]
        gpres = [g for c in range(NCH) for g in done[c][1]]
        keep, send, done["sums"] = grad_weight(chain, flats, gpres)
        got = dp_swap(send, 0)
        yield
        for step in (1, 2):
            keep, send = add_rows(chain, keep, got, True)
            got = dp_swap(send, step)
            yield
        done["w"] = add_out(chain, keep, got)
        yield

    def sums():
        x = done["sums"]
        for step in range(3):
            got = dp_swap(x, step)
            yield
            if step < 2:
                x = add_rows(chain, x, got, dtype=f32)
        done["sums"] = split_sums(chain, x, got)
        yield

    steps = {c: chunk(c) for c in range(NCH)}
    steps["w"], steps["s"] = weight(), sums()
    for who in ORDER:
        next(steps[who])
    grad_p, grad_b = done["sums"]
    return done["gx"], done["w"], grad_p.T, grad_b.reshape(H)


def solution(mesh):
    in_specs = (P("dp", "tok", None), P("tok", None), P("tok", None), P(), P("dp", None))
    out_specs = (P("dp", "tok", None), P(("tok", "dp"), None), P("tok", None), P())
    return jax.shard_map(
        per_device, mesh=mesh, in_specs=in_specs, out_specs=out_specs, check_vma=False
    )
```

```python
import jax
import jax.numpy as jnp
from jax import lax
from jax.experimental import pallas as pl
from jax.experimental.pallas import tpu as pltpu
from jax.sharding import PartitionSpec as P

f32 = jnp.float32
bf = jnp.bfloat16
T, K, D, H = 64, 32, 256, 1024
EB = 16
PITCH = T + 1
NCH = 2
ORDERS = (("AZB", "BZA"), ("AZB", "BZA"))
DP_ORDERS = ("ABZ", "BAZ")
ORDER = (
    0, 0, 0, 1, 1, 1, 0, 1, 0, 0, 1, 0, 1, 1, 0, 1, 0, 0, 0, 0,
    1, 1, 0, 1, 1, 0, 1, 0, 0, 1, 0, 1, 0, 1, 1, 1, 0, "w", 1, 0,
    0, 1, 0, 1, 1, 0, "w", 0, 1, 0, 0, 0, "w", 1, 1, 1, "s", 1, "s", 0,
    "s", 1, "w", "s",
)


class Chain:
    def __init__(self):
        self.last = []


def call(chain, body, name, outs, scratch, smem=(), vmem=(), far=(), alias=None):
    specs = [pl.BlockSpec(memory_space=pltpu.SMEM)] * len(smem)
    specs += [pl.BlockSpec(memory_space=pltpu.VMEM)] * len(vmem)
    specs += [pl.BlockSpec(memory_space=pl.ANY)] * (len(far) + len(chain.last))
    vmem = [pltpu.with_memory_space_constraint(a, pltpu.VMEM) if a.size > 100000 else a for a in vmem]
    far = [pltpu.with_memory_space_constraint(a, pltpu.HBM) for a in far]
    ins, skip = len(smem) + len(vmem) + len(far), len(chain.last)

    def run(*refs):
        body(*refs[:ins], *refs[ins + skip :])

    def place(out):
        return pl.BlockSpec(memory_space=pltpu.VMEM if isinstance(out, jax.ShapeDtypeStruct) else pl.ANY)

    result = pl.pallas_call(
        run,
        out_shape=outs,
        in_specs=specs,
        out_specs=[place(out) for out in outs],
        scratch_shapes=scratch,
        input_output_aliases=alias or {},
        compiler_params=pltpu.CompilerParams(vmem_limit_bytes=8 * 1024 * 1024),
        cost_estimate=pl.CostEstimate(flops=int(2e10), bytes_accessed=1000, transcendentals=0),
        name=name,
    )(*smem, *vmem, *far, *chain.last)
    chain.last = [result[-1]]
    return result


def shape(*dims, dtype=bf):
    return jax.ShapeDtypeStruct(dims, dtype)


def compress(chain, x, pt, tbl, blk):
    n = tbl.shape[0]

    def body(tbl, blk, pt, x, xv, out, sem, pt4):
        def copy(i):
            return pltpu.make_async_copy(x.at[pl.ds((blk[0] + i) * EB, EB)], xv.at[pl.ds(i * EB, EB)], sem.at[i])

        for i in range(n // EB):
            copy(i).start()

        wide = jnp.concatenate([pt[...].astype(f32)] * 4, axis=1)
        lane = lax.broadcasted_iota(jnp.int32, (K, 4 * T), 1) // T
        for j in range(4):
            pt4[K * j : K * j + K, :] = jnp.where(lane == j, wide, 0.0).astype(bf)

        @pl.loop(0, n // EB)
        def _(i):
            copy(i).wait()
            for g in range(EB // 4):
                x4 = xv[pl.ds(i * EB + 4 * g, 4)].reshape(4 * T, D)
                r = jnp.dot(pt4[...], x4, preferred_element_type=f32).astype(bf)
                for j in range(4):
                    out[tbl[i * EB + 4 * g + j]] = r[K * j : K * j + K]

    outs = [shape(n, T, D), shape(n, K, D)]
    scratch = [pltpu.SemaphoreType.DMA((n // EB,)), pltpu.VMEM((4 * K, 4 * T), bf)]
    return call(chain, body, "compress", outs, scratch, [tbl, blk], [pt], [x])


def field(chain, x, comp, w, tbl, perm):
    n = tbl.shape[0]

    def body(tbl, perm, comp, x, w, flatp, hidden, sc, flat):
        lane = lax.broadcasted_iota(jnp.int32, (EB, 128), 1) // K

        @pl.loop(0, n // EB)
        def _(i):
            for e in range(EB):
                c = comp[tbl[i * EB + e]]
                sc[PITCH * e : PITCH * e + T, :K] = lax.dot_general(
                    x[i * EB + e], c, (((1,), (1,)), ((), ())), preferred_element_type=f32
                )
            rows = pl.ds(pl.multiple_of(i * EB, EB), EB)
            for g in range(T // 4):
                acc = sc[pl.ds(4 * g, EB, stride=PITCH), :]
                for j in range(1, 4):
                    v = pltpu.roll(sc[pl.ds(4 * g + j, EB, stride=PITCH), :], K * j, 1)
                    acc = jnp.where(lane == j, v, acc)
                flat[rows, 128 * g : 128 * g + 128] = acc.astype(bf)
            for j in range(8):
                at = pl.ds(pl.multiple_of(perm[j] * 256, 256), 256)
                flatp[rows, 256 * j : 256 * j + 256] = flat[rows, at]

        for j in range(H // 256):
            at = slice(256 * j, 256 * j + 256)
            hidden[:, at] = jnp.dot(flat[...], w[:, at], preferred_element_type=f32).astype(bf)

    scratch = [pltpu.VMEM((EB * PITCH, 128), f32), pltpu.VMEM((n, T * K), bf)]
    return call(chain, body, "field", [shape(n, T * K), shape(n, H)], scratch, [tbl, perm], [comp, x, w])


def spread(df, rows, sc, tail=None):
    lane = lax.broadcasted_iota(jnp.int32, (EB, 128), 1)
    for g in range(T // 4):
        v = df[rows, 128 * g : 128 * g + 128].astype(f32)
        for j in range(4):
            w = v if j == 0 else pltpu.roll(v, 128 - K * j, 1)
            if tail is not None:
                w = jnp.where(lane < K, w, tail[4 * g + j : 4 * g + j + 1, :])
            sc[pl.ds(4 * g + j, EB, stride=PITCH), :] = w


def silu_grad(value):
    sig = jax.nn.sigmoid(value)
    return sig * (1.0 + value * (1.0 - sig))


def grad_compress(chain, x, pre, up, bias, w, tbl, blk):
    n = tbl.shape[0]

    def body(tbl, blk, pre, up, bias, x, w, gpre, df, out, sc):
        @pl.loop(0, n // EB)
        def _(i):
            rows = pl.ds(pl.multiple_of(i * EB, EB), EB)
            u = up[pl.ds(pl.multiple_of((blk[0] + i) * EB, EB), EB), :].astype(f32)
            gpre[rows, :] = (u * silu_grad(pre[rows, :].astype(f32) + bias[...])).astype(bf)

        for j in range(T * K // 256):
            at = slice(256 * j, 256 * j + 256)
            df[:, at] = lax.dot_general(
                gpre[...], w[at, :], (((1,), (1,)), ((), ())), preferred_element_type=f32
            ).astype(bf)

        @pl.loop(0, n // EB)
        def _(i):
            spread(df, pl.ds(pl.multiple_of(i * EB, EB), EB), sc)
            for e in range(EB):
                s = sc[PITCH * e : PITCH * e + T, :K].astype(bf)
                r = lax.dot_general(s, x[i * EB + e], (((0,), (0,)), ((), ())), preferred_element_type=f32)
                out[tbl[i * EB + e]] = r.astype(bf)

    outs = [shape(n, H), shape(n, T * K), shape(n, K, D)]
    scratch = [pltpu.VMEM((EB * PITCH, 128), f32)]
    return call(chain, body, "grad_compress", outs, scratch, [tbl, blk], [pre, up, bias, x, w])


def grad_weight(chain, flats, gpres):
    m = T * K // 2

    def body(*refs):
        ins, (keep, send, sums) = refs[:-3], refs[-3:]
        flats, gpres = ins[: len(ins) // 2], ins[len(ins) // 2 :]
        g = jnp.concatenate([r[...] for r in gpres], axis=0)
        for j in range(8):
            f = jnp.concatenate([r[:, 256 * j : 256 * j + 256] for r in flats], axis=0)
            r = lax.dot_general(f, g, (((0,), (0,)), ((), ())), preferred_element_type=f32).astype(bf)
            out, at = (keep, 256 * j) if j < 4 else (send, 256 * j - m)
            out[at : at + 256, :] = r
        sums[...] = jnp.zeros_like(sums)
        total = jnp.sum(g.astype(f32), axis=0, keepdims=True)
        for j in range(H // 128):
            sums[K + j : K + j + 1, :] = total[:, 128 * j : 128 * j + 128]

    outs = [shape(m, H), shape(m, H), shape(K + H // 128, 128, dtype=f32)]
    return call(chain, body, "grad_weight", outs, [], [], [*flats, *gpres])


def grad_projection(chain, x, dcomp, sums, tbl):
    n = tbl.shape[0]

    def body(tbl, dcomp, x, sums, out):
        out[...] = sums[...]

        @pl.loop(0, n // EB)
        def _(i):
            acc = out[:K, :T]
            for e in range(EB):
                acc = acc + lax.dot_general(
                    dcomp[tbl[i * EB + e]], x[i * EB + e], (((1,), (1,)), ((), ())), preferred_element_type=f32
                )
            out[:K, :T] = acc

    return call(chain, body, "grad_projection", [shape(*sums.shape, dtype=f32)], [], [tbl], [dcomp, x, sums])[0]


def grad_tokens(chain, df, comp, dcomp, pt, gx, dims, tbl, blk):
    n = tbl.shape[0]
    far = [] if gx is None else [gx]

    def body(tbl, blk, df, comp, dcomp, pt, *rest):
        out, mark, ov, sem, sc, tail = rest[len(far) :]
        p = pt[...].astype(f32).T
        tail[:, : 2 * K] = jnp.concatenate([p, p], axis=1)
        mark[...] = jnp.zeros_like(mark)

        def copy(i):
            return pltpu.make_async_copy(ov.at[pl.ds(i * EB, EB)], out.at[pl.ds((blk[0] + i) * EB, EB)], sem.at[i])

        @pl.loop(0, n // EB)
        def _(i):
            spread(df, pl.ds(pl.multiple_of(i * EB, EB), EB), sc, tail)
            for e in range(EB):
                s = sc[PITCH * e : PITCH * e + T, : 2 * K].astype(bf)
                at = tbl[i * EB + e]
                w = jnp.concatenate([comp[at], dcomp[at]], axis=0)
                ov[i * EB + e] = jnp.dot(s, w, preferred_element_type=f32).astype(bf)
            copy(i).start()

        for i in range(n // EB):
            copy(i).wait()

    outs = [pltpu.HBM(dims, bf), shape(8, 128, dtype=f32)]
    scratch = [pltpu.VMEM((n, T, D), bf), pltpu.SemaphoreType.DMA((n // EB,)), pltpu.VMEM((EB * PITCH, 128), f32)]
    scratch += [pltpu.VMEM((T, 128), f32)]
    alias = {6: 0} if far else None
    return call(chain, body, "grad_tokens", outs, scratch, [tbl, blk], [df, comp, dcomp, pt], far, alias)[0]


def add_rows(chain, a, b, cut=False, dtype=bf):
    n, rest = a.shape[0], a.shape[1:]
    m = n // 2 if cut else n
    step = 10 if len(rest) == 2 else 16 if a.dtype == bf else 8

    def body(a, b, *outs):
        for k, out in enumerate(outs):

            @pl.loop(0, m // step)
            def _(i):
                to = pl.multiple_of(i * step, step)
                at = pl.ds(pl.multiple_of(k * m + i * step, step), step)
                out[pl.ds(to, step)] = (a[at].astype(f32) + b[at].astype(f32)).astype(out.dtype)

    outs = call(chain, body, "add", [shape(m, *rest, dtype=dtype)] * (n // m), [], [], [a, b])
    return outs if cut else outs[0]


def add_out(chain, a, b):
    n, m, step = a.shape[0], a.shape[1], 64

    def body(a, b, out, mark, ov, sem):
        mark[...] = jnp.zeros_like(mark)
        copies = []
        for i in range(n // step):
            at = pl.ds(i * step, step)
            ov[at] = a[at].astype(f32) + b[at].astype(f32)
            copies.append(pltpu.make_async_copy(ov.at[at], out.at[at], sem.at[i]))
            copies[-1].start()
        for copy in copies:
            copy.wait()

    outs = [pltpu.HBM((n, m), f32), shape(8, 128, dtype=f32)]
    scratch = [pltpu.VMEM((n, m), f32), pltpu.SemaphoreType.DMA((n // step,))]
    return call(chain, body, "add", outs, scratch, [], [a, b])[0]


def split_sums(chain, a, b):
    def body(a, b, gp, gb):
        gp[...] = a[:K, :T] + b[:K, :T]
        gb[...] = a[K:, :] + b[K:, :]

    outs = [shape(K, T, dtype=f32), shape(H // 128, 128, dtype=f32)]
    return call(chain, body, "add", outs, [], [], [a, b])


def join_rows(chain, a, b):
    n, rest = a.shape[0], a.shape[1:]

    def body(a, b, out):
        @pl.loop(0, n // 10)
        def _(i):
            out[pl.ds(i * 10, 10)] = a[pl.ds(i * 10, 10)]
            out[pl.ds(n + i * 10, 10)] = b[pl.ds(i * 10, 10)]

    return call(chain, body, "join", [shape(2 * n, *rest)], [], [], [a, b])[0]


def tok_bits(i):
    x = i // 4
    g = x ^ (x >> 1)
    return {"A": g & 1, "B": g >> 1, "Z": (i >> 1) & 1}


def tok_flip(i, d):
    x = i // 4
    return {"A": (x ^ 1) * 4 + i % 4, "B": (3 - x) * 4 + i % 4, "Z": i ^ 2, "C": i ^ 1}[d]


def dp_bits(i):
    y = i // 2
    g = y ^ (y >> 1)
    return {"A": g & 1, "B": g >> 1, "Z": i & 1}


def dp_flip(i, d):
    y = i // 2
    return {"A": (y ^ 1) * 2 + i % 2, "B": (3 - y) * 2 + i % 2, "Z": i ^ 1}[d]


def place(bits, order):
    return bits[order[0]] * 4 + bits[order[1]] * 2 + bits[order[2]]


def tok_swap(x, step, orders):
    if step == "C":
        pairs = [(i, tok_flip(i, "C")) for i in range(16)]
    else:
        pairs = [(i, tok_flip(i, orders[i & 1][step])) for i in range(16)]
    return lax.ppermute(x, "tok", pairs)


def dp_swap(x, step):
    pairs = []
    for d in range(8):
        for t in range(16):
            pairs.append((d * 16 + t, dp_flip(d, DP_ORDERS[t & 1][step]) * 16 + t))
    return lax.ppermute(x, ("dp", "tok"), pairs)


def per_device(embeddings, projection, mlp_weight, mlp_bias, upstream):
    half = embeddings.shape[0] // NCH // 2
    part = half // 8
    tok = lax.axis_index("tok")
    core = tok & 1
    bits, dbits = tok_bits(tok), dp_bits(lax.axis_index("dp"))
    own = jnp.where(core == 0, place(dbits, DP_ORDERS[0]), place(dbits, DP_ORDERS[1])) ^ jnp.arange(8, dtype=jnp.int32)
    digits = (own >> 2, (own >> 1) & 1, own & 1)
    blocks = []
    for order in DP_ORDERS:
        at = dict(zip(order, digits))
        g = at["A"] + 2 * at["B"]
        blocks.append((g ^ (g >> 1)) * 2 + at["Z"])
    perm = jnp.where(core == 0, blocks[0], blocks[1])

    pt = projection.T
    bias = mlp_bias.reshape(1, H)

    e = jnp.arange(half, dtype=jnp.int32)
    tables, blocks = [], []
    for c in range(NCH):
        tabs = [((e // part) ^ place(bits, ORDERS[c][h])) * part + e % part for h in range(2)]
        tables.append((jnp.where(core == 0, tabs[0], tabs[1]), jnp.where(core == 0, tabs[1], tabs[0])))
        first = c * 2 * half // EB
        blocks.append(((first + core * (half // EB)).reshape(1), (first + (1 - core) * (half // EB)).reshape(1)))

    chain = Chain()
    chain.last = [perm, bias, *(a for c in range(NCH) for pair in (tables[c], blocks[c]) for a in pair)]
    done = {}

    def total(swap, mine, got):
        for step in range(3):
            mine, send = add_rows(chain, mine, got, True)
            got = swap(send, step)
            yield
        mine = add_rows(chain, mine, got)
        for step in (2, 1, 0):
            got = swap(mine, step)
            yield
            mine = join_rows(chain, mine, got)
        return mine

    def chunk(c):
        tbl, blk = tables[c], blocks[c]

        def swap(x, step):
            return tok_swap(x, step, ORDERS[c])

        x1, other = compress(chain, embeddings, pt, tbl[1], blk[1])
        got = swap(other, "C")
        yield
        x0, mine = compress(chain, embeddings, pt, tbl[0], blk[0])
        yield
        mine = yield from total(swap, mine, got)
        other = swap(mine, "C")
        comp = (mine, other)
        yield
        f0, h0 = field(chain, x0, mine, mlp_weight, tbl[0], perm)
        yield
        f1, h1 = field(chain, x1, other, mlp_weight, tbl[1], perm)
        got = swap(h1, "C")
        yield
        pre = h0
        for step in range(3):
            pre = add_rows(chain, pre, got)
            got = swap(pre, step)
            yield
        pre = add_rows(chain, pre, got)
        got = swap(pre, "C")
        yield
        g1, d1, other = grad_compress(chain, x1, got, upstream, bias, mlp_weight, tbl[1], blk[1])
        got = swap(other, "C")
        yield
        g0, d0, mine = grad_compress(chain, x0, pre, upstream, bias, mlp_weight, tbl[0], blk[0])
        done[c] = ((f0, f1), (g0, g1))
        yield
        mine = yield from total(swap, mine, got)
        other = swap(mine, "C")
        dcomp = (mine, other)
        yield
        done["sums"] = grad_projection(chain, x0, mine, done["sums"], tbl[0])
        yield
        done["sums"] = grad_projection(chain, x1, other, done["sums"], tbl[1])
        yield
        for h, d in ((0, d0), (1, d1)):
            done["gx"] = grad_tokens(
                chain, d, comp[h], dcomp[h], pt, done.get("gx"), embeddings.shape, tbl[h], blk[h]
            )
            yield

    def weight():
        flats = [f for c in range(NCH) for f in done[c][0]]
        gpres = [g for c in range(NCH) for g in done[c][1]]
        keep, send, done["sums"] = grad_weight(chain, flats, gpres)
        got = dp_swap(send, 0)
        yield
        for step in (1, 2):
            keep, send = add_rows(chain, keep, got, True)
            got = dp_swap(send, step)
            yield
        done["w"] = add_out(chain, keep, got)
        yield

    def sums():
        x = done["sums"]
        for step in range(3):
            got = dp_swap(x, step)
            yield
            if step < 2:
                x = add_rows(chain, x, got, dtype=f32)
        done["sums"] = split_sums(chain, x, got)
        yield

    steps = {c: chunk(c) for c in range(NCH)}
    steps["w"], steps["s"] = weight(), sums()
    for who in ORDER:
        next(steps[who])
    grad_p, grad_b = done["sums"]
    return done["gx"], done["w"], grad_p.T, grad_b.reshape(H)


def solution(mesh):
    in_specs = (P("dp", "tok", None), P("tok", None), P("tok", None), P(), P("dp", None))
    out_specs = (P("dp", "tok", None), P(("tok", "dp"), None), P("tok", None), P())
    return jax.shard_map(
        per_device, mesh=mesh, in_specs=in_specs, out_specs=out_specs, check_vma=False
    )
```
